256 devices in a mesh: tile: 32 (over z, y_lo, core), freq: 8 (over y_hi, x).
Axes of the slice: x: 4, y: 4 (y_hi: 2, y_lo: 2; y = y_hi * 2 + y_lo), z: 8, core: 2. Of those that a mesh axis runs over, the one named last changes fastest.
Arguments:
- wavefield: bfloat16 [8, 2, 16384, 256], P('freq', None, 'tile'), may hold values from -6 to 6
- row_factors: bfloat16 [8, 2, 32768, 1024], P('freq', None, 'tile'), may hold values from -0.125 to 0.125
- col_factors: bfloat16 [8, 2, 16384, 2048], P('freq', None, 'tile'), may hold values from -0.1875 to 0.1875
- window_index: int32 [256], replicated, may hold values from 1 to 15
Outputs:
- adjoint_field: float32 [8, 2, 16384, 256], P('freq', None, 'tile')
The draws below stay inside these ranges and needn't reach their ends.
All inputs are finite; a program needn't handle non-finite values.
Results may differ from the reference program's by a relative error of at most 0.0038.
Values may be sent and summed in bfloat16 or wider, within the bound.
A program may use at most 128 MiB of HBM per device.

```python
import math
import jax
import jax.numpy as jnp
from jax import lax

FREQS = 8
NR = 32768
NS = 16384
TS = 512
RANK = 32
VP = 256
NT = 16
RTILES = 64
CTILES = 32


def set_ends(values, stream_key, low, top_value):
    shape = values.shape
    spot = [jax.random.randint(jax.random.fold_in(stream_key, axis), (), 0, shape[axis]) for axis in range(len(shape))]
    values = values.at[tuple(spot)].set(low)
    longest = shape.index(max(shape))
    spot[longest] = (spot[longest] + 1) % shape[longest]
    return values.at[tuple(spot)].set(top_value)


def level_of(key, shape, shards, low, top_value):
    gain = 1.0
    for dim, parts in shards:
        steps = jax.random.uniform(jax.random.fold_in(jax.random.fold_in(key, 6), dim), (parts,), jnp.float32, low / len(shards), top_value / len(shards))
        gain = gain * jnp.repeat(jnp.exp(steps), shape[dim] // parts).reshape((-1,) + (1,) * (len(shape) - 1 - dim))
    return gain


def centred(stream_key, dims, deviation, most, pieces=(), held_as=jnp.bfloat16):
    entries = jax.random.normal(stream_key, dims, jnp.float32) * deviation
    if len(pieces) > 0:
        entries = level_of(stream_key, dims, pieces, -0.22, 0.18) * entries
    return jnp.clip(entries, min=-most, max=most).astype(held_as)


def setup_inputs(seed: int = 0) -> dict:
    key_of = jax.random.split(jax.random.key(seed), 5)
    wavefield = centred(key_of[0], (FREQS, 2, NS, VP), 1.0, 6.0, ((0, 8), (2, 32)))
    row_factors = centred(key_of[1], (FREQS, 2, NR, CTILES * RANK), (2 * CTILES * RANK) ** -0.5, 0.125, ((0, 8), (2, 32)))
    col_factors = centred(key_of[2], (FREQS, 2, NS, RTILES * RANK), (2 * TS) ** -0.5, 0.1875, ((0, 8), (2, 32)))
    window_index = set_ends(jax.random.randint(key_of[3], (VP,), 1, NT), jax.random.fold_in(key_of[3], 1), 1, NT - 1).astype(jnp.int32)
    return {"wavefield": wavefield, "row_factors": row_factors, "col_factors": col_factors, "window_index": window_index}


def angles(freq_ids):
    times = lax.broadcasted_iota(jnp.int32, (NT, freq_ids.shape[0]), 0)
    return (math.pi / NT) * ((2 * freq_ids[None, :] + 1) * times).astype(jnp.float32)


def forward_one(packed):
    wave, row_f, col_f = packed
    col_view = col_f.astype(jnp.float32).reshape(2, CTILES, TS, RTILES * RANK)
    wave_view = wave.astype(jnp.float32).reshape(2, CTILES, TS, VP)

    def project(left, right):
        return jnp.einsum("csa,csv->cav", left, right)

    real_part = project(col_view[0], wave_view[0]) + project(col_view[1], wave_view[1])
    imag_part = project(col_view[0], wave_view[1]) - project(col_view[1], wave_view[0])
    coeffs = jnp.stack([real_part, imag_part]).astype(jnp.bfloat16).reshape(2, CTILES, RTILES, RANK, VP)
    coeffs = jnp.transpose(coeffs, (0, 2, 1, 3, 4)).reshape(2, RTILES, CTILES * RANK, VP).astype(jnp.float32)
    row_view = row_f.astype(jnp.float32).reshape(2, RTILES, TS, CTILES * RANK)

    def expand(left, right):
        return jnp.einsum("isa,iav->isv", left, right)

    real_out = expand(row_view[0], coeffs[0]) - expand(row_view[1], coeffs[1])
    imag_out = expand(row_view[0], coeffs[1]) + expand(row_view[1], coeffs[0])
    return jnp.stack([real_out, imag_out]).astype(jnp.bfloat16).reshape(2, NR, VP)


def adjoint_one(packed):
    filtered, row_f, col_f = packed
    row_view = row_f.astype(jnp.float32).reshape(2, RTILES, TS, CTILES * RANK)
    filt_view = filtered.astype(jnp.float32).reshape(2, RTILES, TS, VP)

    def contract(left, right):
        return jnp.einsum("isa,isv->iav", left, right)

    real_part = contract(row_view[0], filt_view[0]) + contract(row_view[1], filt_view[1])
    imag_part = contract(row_view[0], filt_view[1]) - contract(row_view[1], filt_view[0])
    returned = jnp.stack([real_part, imag_part]).astype(jnp.bfloat16).reshape(2, RTILES, CTILES, RANK, VP)
    returned = jnp.transpose(returned, (0, 2, 1, 3, 4)).reshape(2, CTILES, RTILES * RANK, VP).astype(jnp.float32)
    col_view = col_f.astype(jnp.float32).reshape(2, CTILES, TS, RTILES * RANK)

    def spread(left, right):
        return jnp.einsum("csa,cav->csv", left, right)

    real_out = spread(col_view[0], returned[0]) - spread(col_view[1], returned[1])
    imag_out = spread(col_view[0], returned[1]) + spread(col_view[1], returned[0])
    return jnp.stack([real_out, imag_out]).reshape(2, NS, VP)


def reference(wavefield, row_factors, col_factors, window_index):
    spectra = lax.map(forward_one, (wavefield, row_factors, col_factors))
    freq_ids = lax.iota(jnp.int32, FREQS)
    phases = angles(freq_ids)
    cosine = 0.25 * jnp.cos(phases)
    sine = 0.25 * jnp.sin(phases)
    high = lax.Precision.HIGHEST
    timed = jnp.einsum("tk,krv->trv", cosine, spectra[:, 0].astype(jnp.float32), precision=high)
    timed = timed - jnp.einsum("tk,krv->trv", sine, spectra[:, 1].astype(jnp.float32), precision=high)
    time_mask = (lax.broadcasted_iota(jnp.int32, (NT, VP), 0) < window_index[None, :]).astype(jnp.float32)
    windowed = timed * time_mask[:, None, :]
    real_part = jnp.einsum("tk,trv->krv", cosine, windowed, precision=high)
    imag_part = -jnp.einsum("tk,trv->krv", sine, windowed, precision=high)
    filtered = jnp.stack([real_part, imag_part], 1).astype(jnp.bfloat16)
    return lax.map(adjoint_one, (filtered, row_factors, col_factors))
```

```python
import functools
import math

import jax
import jax.numpy as jnp
import numpy as np
from jax import lax
from jax.experimental import pallas as pl
from jax.experimental.pallas import tpu as pltpu
from jax.sharding import PartitionSpec as P

TS = 512
RANK = 32
NT = 16
FREQS = 8
ZN = 8
XN = 4
VP = 256
LANES = 128
HALVES = 2
ROW_TILES = 2
SHARE = TS // FREQS
GROUP = 4 * ROW_TILES
MESH = pl.DeviceIdType.MESH
F32 = jnp.float32
BF16 = jnp.bfloat16


def transform_matrices():
    times, freqs = np.meshgrid(np.arange(NT), np.arange(FREQS), indexing="ij")
    angles = math.pi / NT * (2 * freqs + 1) * times
    eye = np.eye(16)
    forward = np.concatenate([np.kron(0.25 * np.cos(angles), eye), np.kron(-0.25 * np.sin(angles), eye)], 1)
    both = np.stack([forward, forward.T])
    high = both.astype(BF16)
    low = (both - high.astype(np.float64)).astype(BF16)
    return np.stack([high, low])


def zdelta(k):
    return jnp.where(k % 2 == 1, (k + 1) // 2, ZN - k // 2)


def dot(left, right):
    return jnp.dot(left, right, preferred_element_type=F32)


def dot_t(left, right):
    return lax.dot_general(left, right, (((0,), (0,)), ((), ())), preferred_element_type=F32)


def turned(pair, sign):
    re, im = pair[:, :LANES], pair[:, LANES:]
    return jnp.concatenate([-im, re] if sign > 0 else [im, -re], 1)


def kernel(
    wave_hbm, row_hbm, col_hbm, index_ref, mats_ref, out_ref,
    wave, row, col, x_one, x_two,
    c_send, c_recv, y_send, y_recv, f_send, f_recv, r_send, r_recv,
    load_wave, load_row, load_col,
    send_a, send_b, send_c, send_d, recv_a, recv_b, recv_c, recv_d,
):
    me, freq = lax.axis_index("tile"), lax.axis_index("freq")
    my_z, my_y, my_core = me // 4, (me // 2) % 2, me % 2

    loads = [
        pltpu.make_async_copy(wave_hbm.at[0], wave, load_wave),
        pltpu.make_async_copy(col_hbm.at[0], col, load_col),
        pltpu.make_async_copy(row_hbm.at[0], row, load_row),
    ]
    for load in loads:
        load.start()

    def tile_peer(k, q):
        z = (my_z + zdelta(k)) % ZN
        return z * 4 + ((my_y + q // 2) % 2) * 2 + (my_core + q % 2) % 2

    def freq_peer(n):
        return (freq + n) % FREQS

    barrier = pltpu.get_barrier_semaphore()
    for q in range(1, 4):
        pl.semaphore_signal(barrier, inc=1, device_id={"tile": tile_peer(0, q)}, device_id_type=MESH)

    def greet(k, carry):
        for q in range(4):
            pl.semaphore_signal(barrier, inc=1, device_id={"tile": tile_peer(k, q)}, device_id_type=MESH)
        return carry

    lax.fori_loop(1, ZN, greet, 0)
    for n in range(1, FREQS):
        pl.semaphore_signal(barrier, inc=1, device_id={"freq": freq_peer(n)}, device_id_type=MESH)

    loads[0].wait()
    for h in range(HALVES):
        xr = wave[0, :, h * LANES : (h + 1) * LANES]
        xi = wave[1, :, h * LANES : (h + 1) * LANES]
        x_one[:, 2 * h * LANES : (2 * h + 1) * LANES] = xr
        x_one[:, (2 * h + 1) * LANES : (2 * h + 2) * LANES] = xi
        x_two[:, 2 * h * LANES : (2 * h + 1) * LANES] = xi
        x_two[:, (2 * h + 1) * LANES : (2 * h + 2) * LANES] = -xr

    def copy_a(h, peer, k, q):
        return pltpu.make_async_remote_copy(
            src_ref=c_send.at[h, pl.ds(ROW_TILES * peer, ROW_TILES)],
            dst_ref=c_recv.at[h, :, me],
            send_sem=send_a.at[h, 4 * k + q],
            recv_sem=recv_a.at[h],
            device_id={"tile": peer},
            device_id_type=MESH,
        )

    def copy_d(h, peer, k, q):
        return pltpu.make_async_remote_copy(
            src_ref=r_send.at[h, :, peer],
            dst_ref=r_recv.at[h, pl.ds(ROW_TILES * me, ROW_TILES)],
            send_sem=send_d.at[h, 4 * k + q],
            recv_sem=recv_d.at[h, my_z],
            device_id={"tile": peer},
            device_id_type=MESH,
        )

    def own_a(h):
        return pltpu.make_async_copy(
            c_send.at[h, pl.ds(ROW_TILES * me, ROW_TILES)], c_recv.at[h, :, me], recv_a.at[h]
        )

    def own_d(h):
        return pltpu.make_async_copy(
            r_send.at[h, :, me], r_recv.at[h, pl.ds(ROW_TILES * me, ROW_TILES)], recv_d.at[h, my_z]
        )

    def copy_b(h, n):
        peer = freq_peer(n)
        return pltpu.make_async_remote_copy(
            src_ref=y_send.at[h, :, peer],
            dst_ref=y_recv.at[h, :, freq],
            send_sem=send_b.at[h, n],
            recv_sem=recv_b.at[h],
            device_id={"freq": peer},
            device_id_type=MESH,
        )

    def copy_c(h, n):
        peer = freq_peer(n)
        return pltpu.make_async_remote_copy(
            src_ref=f_send.at[h, :, peer],
            dst_ref=f_recv.at[h, :, freq],
            send_sem=send_c.at[h, n],
            recv_sem=recv_c.at[h],
            device_id={"freq": peer},
            device_id_type=MESH,
        )

    def groups(step, first=1):
        def body(k, carry):
            for q in range(4):
                step(k, q)
            return carry

        lax.fori_loop(first, ZN, body, 0)
        for q in range(1, 4):
            step(0, q)

    def project(k):
        z = (my_z + zdelta(k)) % ZN
        columns = pl.ds(pl.multiple_of(z * 256, 256), 256)
        value = dot_t(col[0, :, columns], x_one[...]) + dot_t(col[1, :, columns], x_two[...])
        value = value.astype(BF16)
        for h in range(HALVES):
            c_send[h, pl.ds(GROUP * z, GROUP)] = value[:, 256 * h : 256 * (h + 1)].reshape(GROUP, RANK, 256)

    loads[1].wait()
    with jax.named_scope("entry_barrier"):
        pl.semaphore_wait(barrier, 31 + 7)

    with jax.named_scope("coeffs_and_send"):

        def first(k, carry):
            project(k)
            for q in range(4):
                copy_a(0, tile_peer(k, q), k, q).start()
            return carry

        lax.fori_loop(1, ZN, first, 0)
        project(0)
        for q in range(1, 4):
            copy_a(0, tile_peer(0, q), 0, q).start()
        for h in range(HALVES):
            own_a(h).start()

    with jax.named_scope("second_coeffs_send"):

        def second(k, q):
            peer = tile_peer(k, q)
            copy_a(0, peer, k, q).wait_send()
            copy_a(1, peer, k, q).start()

        groups(second)

    loads[2].wait()

    def spectra(h):
        pltpu.make_async_copy(c_recv.at[h], c_recv.at[h], recv_a.at[h]).wait()
        for i in range(ROW_TILES):
            c_one = c_recv[h, i].reshape(32 * RANK, 256)
            rows = slice(i * TS, (i + 1) * TS)
            value = dot(row[0, rows], c_one) + dot(row[1, rows], turned(c_one, 1))
            y_send[h, i] = value.astype(BF16).reshape(FREQS, SHARE, 256)
        for n in range(1, FREQS):
            copy_b(h, n).start()
        pltpu.make_async_copy(y_send.at[h, :, freq], y_recv.at[h, :, freq], recv_b.at[h]).start()

    def window(h):
        pltpu.make_async_copy(y_recv.at[h], y_recv.at[h], recv_b.at[h]).wait()
        times = lax.broadcasted_iota(jnp.int32, (256, LANES), 0) // 16
        kept = times < index_ref[:, h * LANES : (h + 1) * LANES]
        kept = jnp.concatenate([kept.astype(F32)] * 2, 1) > 0.5
        for i in range(ROW_TILES):
            for b in range(2):
                blocks = []
                for u in range(2):
                    rows = slice((2 * b + u) * 16, (2 * b + u + 1) * 16)
                    block = y_recv[h, i, :, rows].reshape(FREQS * 16, 256)
                    blocks.append(jnp.concatenate([block[:, :LANES], block[:, LANES:]], 0))
                block = jnp.concatenate(blocks, 1)
                timed = dot(mats_ref[0, 0], block) + dot(mats_ref[1, 0], block)
                timed = jnp.where(kept, timed, 0.0)
                high = timed.astype(BF16)
                low = (timed - high.astype(F32)).astype(BF16)
                value = dot(mats_ref[0, 1], high) + (dot(mats_ref[1, 1], high) + dot(mats_ref[0, 1], low))
                value = value.astype(BF16)
                for u in range(2):
                    rows = slice((2 * b + u) * 16, (2 * b + u + 1) * 16)
                    part = value[:, u * LANES : (u + 1) * LANES]
                    f_send[h, i, :, rows] = jnp.concatenate([part[:128], part[128:]], 1).reshape(FREQS, 16, 256)
        for n in range(1, FREQS):
            copy_c(h, n).start()
        pltpu.make_async_copy(f_send.at[h, :, freq], f_recv.at[h, :, freq], recv_c.at[h]).start()

    def returned(h):
        pltpu.make_async_copy(f_recv.at[h], f_recv.at[h], recv_c.at[h]).wait()
        for i in range(ROW_TILES):
            f_one = f_recv[h, i].reshape(TS, 256)
            rows = slice(i * TS, (i + 1) * TS)
            value = dot_t(row[0, rows], f_one) + dot_t(row[1, rows], turned(f_one, -1))
            r_send[h, i] = value.astype(BF16).reshape(32, RANK, 256)

        def send(k, q):
            peer = tile_peer(k, q)
            (copy_a(1, peer, k, q) if h == 0 else copy_d(0, peer, k, q)).wait_send()
            copy_d(h, peer, k, q).start()

        groups(send)
        own_d(h).start()

    def adjoint(h):
        def step(z, first):
            held = r_recv.at[h, pl.ds(GROUP * z, GROUP)]
            pltpu.make_async_copy(held, held, recv_d.at[h, z]).wait()
            columns = pl.ds(pl.multiple_of(z * 256, 256), 256)
            r_one = held[...].reshape(256, 256)
            value = dot(col[0, :, columns], r_one) + dot(col[1, :, columns], turned(r_one, 1))
            for c in range(2):
                part = value[:, c * LANES : (c + 1) * LANES]
                old = out_ref[0, c, :, h * LANES : (h + 1) * LANES]
                out_ref[0, c, :, h * LANES : (h + 1) * LANES] = part if first else old + part

        step(my_z, True)

        def body(k, carry):
            step((my_z + zdelta(k)) % ZN, False)
            return carry

        lax.fori_loop(1, ZN, body, 0)

    for h in range(HALVES):
        with jax.named_scope("spectra%d" % h):
            spectra(h)
        with jax.named_scope("window%d" % h):
            window(h)
        with jax.named_scope("returned%d" % h):
            returned(h)
    for h in range(HALVES):
        with jax.named_scope("adjoint%d" % h):
            adjoint(h)

    with jax.named_scope("drain"):
        groups(lambda k, q: copy_d(1, tile_peer(k, q), k, q).wait_send())
        for h in range(HALVES):
            for n in range(1, FREQS):
                copy_b(h, n).wait_send()
                copy_c(h, n).wait_send()


def local(mats, wavefield, row_factors, col_factors, window_index):
    vmem = pl.BlockSpec(memory_space=pltpu.VMEM)
    hbm = pl.BlockSpec(memory_space=pl.ANY)
    dma = pltpu.SemaphoreType.DMA
    shape = wavefield.shape
    return pl.pallas_call(
        kernel,
        out_shape=jax.ShapeDtypeStruct(shape, F32),
        in_specs=[hbm, hbm, hbm, vmem, vmem],
        out_specs=vmem,
        scratch_shapes=[
            pltpu.VMEM((2, TS, VP), BF16),
            pltpu.VMEM((2, ROW_TILES * TS, 1024), BF16),
            pltpu.VMEM((2, TS, 2048), BF16),
            pltpu.VMEM((TS, 512), BF16),
            pltpu.VMEM((TS, 512), BF16),
            pltpu.VMEM((HALVES, 64, RANK, 256), BF16),
            pltpu.VMEM((HALVES, ROW_TILES, 32, RANK, 256), BF16),
            pltpu.VMEM((HALVES, ROW_TILES, FREQS, SHARE, 256), BF16),
            pltpu.VMEM((HALVES, ROW_TILES, FREQS, SHARE, 256), BF16),
            pltpu.VMEM((HALVES, ROW_TILES, FREQS, SHARE, 256), BF16),
            pltpu.VMEM((HALVES, ROW_TILES, FREQS, SHARE, 256), BF16),
            pltpu.VMEM((HALVES, ROW_TILES, 32, RANK, 256), BF16),
            pltpu.VMEM((HALVES, 64, RANK, 256), BF16),
            dma, dma, dma,
            dma((HALVES, 32)), dma((HALVES, FREQS)), dma((HALVES, FREQS)), dma((HALVES, 32)),
            dma((HALVES,)), dma((HALVES,)), dma((HALVES,)), dma((HALVES, ZN)),
        ],
        compiler_params=pltpu.CompilerParams(
            collective_id=0, has_side_effects=True, vmem_limit_bytes=56 << 20
        ),
        cost_estimate=pl.CostEstimate(flops=9_000_000_000, bytes_accessed=11_000_000, transcendentals=0),
    )(wavefield, row_factors, col_factors, window_index.reshape(1, VP), jnp.asarray(mats))


def solution(mesh):
    in_specs = (
        P("freq", None, "tile", None),
        P("freq", None, "tile", None),
        P("freq", None, "tile", None),
        P(),
    )
    return jax.shard_map(
        functools.partial(local, transform_matrices()),
        mesh=mesh,
        in_specs=in_specs,
        out_specs=P("freq", None, "tile", None),
        check_vma=False,
    )
```

```python
import functools
import math

import jax
import jax.numpy as jnp
import numpy as np
from jax import lax
from jax.experimental import pallas as pl
from jax.experimental.pallas import tpu as pltpu
from jax.sharding import PartitionSpec as P

TS = 512
RANK = 32
NT = 16
FREQS = 8
ZN = 8
XN = 4
VP = 256
LANES = 128
HALVES = 2
ROW_TILES = 2
SHARE = TS // FREQS
GROUP = 4 * ROW_TILES
CHUNKS = [(h, i) for h in range(HALVES) for i in range(ROW_TILES)]
MESH = pl.DeviceIdType.MESH
F32 = jnp.float32
BF16 = jnp.bfloat16


def transform_matrices():
    times, freqs = np.meshgrid(np.arange(NT), np.arange(FREQS), indexing="ij")
    angles = math.pi / NT * (2 * freqs + 1) * times
    eye = np.eye(16)
    forward = np.concatenate([np.kron(0.25 * np.cos(angles), eye), np.kron(-0.25 * np.sin(angles), eye)], 1)
    both = np.stack([forward, forward.T])
    high = both.astype(BF16)
    low = (both - high.astype(np.float64)).astype(BF16)
    return np.stack([high, low])


def zdelta(k):
    return jnp.where(k % 2 == 1, (k + 1) // 2, ZN - k // 2)


def dot(left, right):
    return jnp.dot(left, right, preferred_element_type=F32)


def dot_t(left, right):
    return lax.dot_general(left, right, (((0,), (0,)), ((), ())), preferred_element_type=F32)


def turned(pair, sign):
    re, im = pair[:, :LANES], pair[:, LANES:]
    return jnp.concatenate([-im, re] if sign > 0 else [im, -re], 1)


def kernel(
    wave_hbm, row_hbm, col_hbm, index_ref, mats_ref, out_ref,
    wave, row, col, x_one, x_two,
    c_send, c_recv, y_send, y_recv, f_send, f_recv, r_send, r_recv,
    load_wave, load_row, load_col,
    send_a, send_b, send_c, send_d, recv_a, recv_b, recv_c, recv_d,
):
    me, freq = lax.axis_index("tile"), lax.axis_index("freq")
    my_z, my_y, my_core = me // 4, (me // 2) % 2, me % 2

    def col_load(k):
        z = (my_z + zdelta(k)) % ZN
        columns = pl.ds(pl.multiple_of(z * 256, 256), 256)
        return pltpu.make_async_copy(col_hbm.at[0, :, :, columns], col.at[:, :, columns], load_col.at[k])

    wave_load = pltpu.make_async_copy(wave_hbm.at[0], wave, load_wave)
    row_load = pltpu.make_async_copy(row_hbm.at[0], row, load_row)
    wave_load.start()
    for k in range(1, ZN):
        col_load(k).start()
    col_load(0).start()

    def tile_peer(k, q):
        z = (my_z + zdelta(k)) % ZN
        return z * 4 + ((my_y + q // 2) % 2) * 2 + (my_core + q % 2) % 2

    def freq_peer(n):
        return (freq + n) % FREQS

    barrier = pltpu.get_barrier_semaphore()
    for q in range(1, 4):
        pl.semaphore_signal(barrier, inc=1, device_id={"tile": tile_peer(0, q)}, device_id_type=MESH)

    def greet(k, carry):
        for q in range(4):
            pl.semaphore_signal(barrier, inc=1, device_id={"tile": tile_peer(k, q)}, device_id_type=MESH)
        return carry

    lax.fori_loop(1, ZN, greet, 0)
    for n in range(1, FREQS):
        pl.semaphore_signal(barrier, inc=1, device_id={"freq": freq_peer(n)}, device_id_type=MESH)

    wave_load.wait()
    for h in range(HALVES):
        xr = wave[0, :, h * LANES : (h + 1) * LANES]
        xi = wave[1, :, h * LANES : (h + 1) * LANES]
        x_one[:, 2 * h * LANES : (2 * h + 1) * LANES] = xr
        x_one[:, (2 * h + 1) * LANES : (2 * h + 2) * LANES] = xi
        x_two[:, 2 * h * LANES : (2 * h + 1) * LANES] = xi
        x_two[:, (2 * h + 1) * LANES : (2 * h + 2) * LANES] = -xr

    def copy_a(h, i, peer, k, q):
        return pltpu.make_async_remote_copy(
            src_ref=c_send.at[h, ROW_TILES * peer + i],
            dst_ref=c_recv.at[h, i, me],
            send_sem=send_a.at[h, i],
            recv_sem=recv_a.at[h, i],
            device_id={"tile": peer},
            device_id_type=MESH,
        )

    def copy_d(h, i, peer, k, q):
        return pltpu.make_async_remote_copy(
            src_ref=r_send.at[h, i, peer],
            dst_ref=r_recv.at[h, ROW_TILES * me + i],
            send_sem=send_d.at[h, i],
            recv_sem=recv_d.at[h, my_z],
            device_id={"tile": peer},
            device_id_type=MESH,
        )

    def own_a(h, i):
        return pltpu.make_async_copy(c_send.at[h, ROW_TILES * me + i], c_recv.at[h, i, me], recv_a.at[h, i])

    def own_d(h, i):
        return pltpu.make_async_copy(r_send.at[h, i, me], r_recv.at[h, ROW_TILES * me + i], recv_d.at[h, my_z])

    def copy_b(h, i, n):
        peer = freq_peer(n)
        return pltpu.make_async_remote_copy(
            src_ref=y_send.at[h, i, peer],
            dst_ref=y_recv.at[h, i, freq],
            send_sem=send_b.at[h, i],
            recv_sem=recv_b.at[h, i],
            device_id={"freq": peer},
            device_id_type=MESH,
        )

    def copy_c(h, i, n):
        peer = freq_peer(n)
        return pltpu.make_async_remote_copy(
            src_ref=f_send.at[h, i, peer],
            dst_ref=f_recv.at[h, i, freq],
            send_sem=send_c.at[h, i],
            recv_sem=recv_c.at[h, i],
            device_id={"freq": peer},
            device_id_type=MESH,
        )

    def groups(step, first=1):
        def body(k, carry):
            for q in range(4):
                step(k, q)
            return carry

        lax.fori_loop(first, ZN, body, 0)
        for q in range(1, 4):
            step(0, q)

    def project(k):
        z = (my_z + zdelta(k)) % ZN
        columns = pl.ds(pl.multiple_of(z * 256, 256), 256)
        value = dot_t(col[0, :, columns], x_one[...]) + dot_t(col[1, :, columns], x_two[...])
        value = value.astype(BF16)
        for h in range(HALVES):
            c_send[h, pl.ds(GROUP * z, GROUP)] = value[:, 256 * h : 256 * (h + 1)].reshape(GROUP, RANK, 256)

    with jax.named_scope("coeffs_and_send"):

        def send_first(k):
            for q in range(4):
                copy_a(0, 0, tile_peer(k, q), k, q).start()

        col_load(1).wait()
        project(1)
        pl.semaphore_wait(barrier, 31 + 7)
        send_first(1)

        def first(k, carry):
            col_load(k).wait()
            project(k)
            send_first(k)
            return carry

        lax.fori_loop(2, ZN, first, 0)
        col_load(0).wait()
        project(0)
        for q in range(1, 4):
            copy_a(0, 0, tile_peer(0, q), 0, q).start()
        row_load.start()

    with jax.named_scope("later_coeffs_send"):
        own_a(0, 0).start()
        for h, i in CHUNKS[1:]:
            groups(lambda k, q: copy_a(h, i, tile_peer(k, q), k, q).start())
            own_a(h, i).start()

    def spectra(h, i):
        if (h, i) == (0, 0):
            row_load.wait()
        pltpu.make_async_copy(c_recv.at[h, i], c_recv.at[h, i], recv_a.at[h, i]).wait()
        c_one = c_recv[h, i].reshape(32 * RANK, 256)
        rows = slice(i * TS, (i + 1) * TS)
        value = dot(row[0, rows], c_one) + dot(row[1, rows], turned(c_one, 1))
        y_send[h, i] = value.astype(BF16).reshape(FREQS, SHARE, 256)
        for n in range(1, FREQS):
            copy_b(h, i, n).start()
        pltpu.make_async_copy(y_send.at[h, i, freq], y_recv.at[h, i, freq], recv_b.at[h, i]).start()

    def window(h, i):
        pltpu.make_async_copy(y_recv.at[h, i], y_recv.at[h, i], recv_b.at[h, i]).wait()
        times = lax.broadcasted_iota(jnp.int32, (256, LANES), 0) // 16
        kept = times < index_ref[:, h * LANES : (h + 1) * LANES]
        kept = jnp.concatenate([kept.astype(F32)] * 2, 1) > 0.5
        for b in range(2):
            blocks = []
            for u in range(2):
                rows = slice((2 * b + u) * 16, (2 * b + u + 1) * 16)
                block = y_recv[h, i, :, rows].reshape(FREQS * 16, 256)
                blocks.append(jnp.concatenate([block[:, :LANES], block[:, LANES:]], 0))
            block = jnp.concatenate(blocks, 1)
            timed = dot(mats_ref[0, 0], block) + dot(mats_ref[1, 0], block)
            timed = jnp.where(kept, timed, 0.0)
            high = timed.astype(BF16)
            low = (timed - high.astype(F32)).astype(BF16)
            value = dot(mats_ref[0, 1], high) + (dot(mats_ref[1, 1], high) + dot(mats_ref[0, 1], low))
            value = value.astype(BF16)
            for u in range(2):
                rows = slice((2 * b + u) * 16, (2 * b + u + 1) * 16)
                part = value[:, u * LANES : (u + 1) * LANES]
                f_send[h, i, :, rows] = jnp.concatenate([part[:128], part[128:]], 1).reshape(FREQS, 16, 256)
        for n in range(1, FREQS):
            copy_c(h, i, n).start()
        pltpu.make_async_copy(f_send.at[h, i, freq], f_recv.at[h, i, freq], recv_c.at[h, i]).start()

    def returned(h, i):
        pltpu.make_async_copy(f_recv.at[h, i], f_recv.at[h, i], recv_c.at[h, i]).wait()
        f_one = f_recv[h, i].reshape(TS, 256)
        rows = slice(i * TS, (i + 1) * TS)
        value = dot_t(row[0, rows], f_one) + dot_t(row[1, rows], turned(f_one, -1))
        r_send[h, i] = value.astype(BF16).reshape(32, RANK, 256)
        groups(lambda k, q: copy_d(h, i, tile_peer(k, q), k, q).start())
        own_d(h, i).start()

    def adjoint(h):
        def step(z, first):
            held = r_recv.at[h, pl.ds(GROUP * z, GROUP)]
            pltpu.make_async_copy(held, held, recv_d.at[h, z]).wait()
            columns = pl.ds(pl.multiple_of(z * 256, 256), 256)
            r_one = held[...].reshape(256, 256)
            value = dot(col[0, :, columns], r_one) + dot(col[1, :, columns], turned(r_one, 1))
            for c in range(2):
                part = value[:, c * LANES : (c + 1) * LANES]
                old = out_ref[0, c, :, h * LANES : (h + 1) * LANES]
                out_ref[0, c, :, h * LANES : (h + 1) * LANES] = part if first else old + part

        step(my_z, True)

        def body(k, carry):
            step((my_z + zdelta(k)) % ZN, False)
            return carry

        lax.fori_loop(1, ZN, body, 0)

    for step in range(len(CHUNKS) + 2):
        for lag, stage in enumerate((spectra, window, returned)):
            if 0 <= step - lag < len(CHUNKS):
                stage(*CHUNKS[step - lag])
    for h in range(HALVES):
        adjoint(h)

    with jax.named_scope("drain"):
        for h, i in CHUNKS:
            sent = r_send.at[h, i, pl.ds(0, 31)]
            pltpu.make_async_copy(sent, sent, send_a.at[h, i]).wait()
            pltpu.make_async_copy(sent, sent, send_d.at[h, i]).wait()
            sent = y_send.at[h, i, pl.ds(0, FREQS - 1)]
            pltpu.make_async_copy(sent, sent, send_b.at[h, i]).wait()
            pltpu.make_async_copy(sent, sent, send_c.at[h, i]).wait()


def local(mats, wavefield, row_factors, col_factors, window_index):
    vmem = pl.BlockSpec(memory_space=pltpu.VMEM)
    hbm = pl.BlockSpec(memory_space=pl.ANY)
    dma = pltpu.SemaphoreType.DMA
    shape = wavefield.shape
    return pl.pallas_call(
        kernel,
        out_shape=pltpu.VMEM(shape, F32),
        in_specs=[hbm, hbm, hbm, vmem, vmem],
        out_specs=vmem,
        scratch_shapes=[
            pltpu.VMEM((2, TS, VP), BF16),
            pltpu.VMEM((2, ROW_TILES * TS, 1024), BF16),
            pltpu.VMEM((2, TS, 2048), BF16),
            pltpu.VMEM((TS, 512), BF16),
            pltpu.VMEM((TS, 512), BF16),
            pltpu.VMEM((HALVES, 64, RANK, 256), BF16),
            pltpu.VMEM((HALVES, ROW_TILES, 32, RANK, 256), BF16),
            pltpu.VMEM((HALVES, ROW_TILES, FREQS, SHARE, 256), BF16),
            pltpu.VMEM((HALVES, ROW_TILES, FREQS, SHARE, 256), BF16),
            pltpu.VMEM((HALVES, ROW_TILES, FREQS, SHARE, 256), BF16),
            pltpu.VMEM((HALVES, ROW_TILES, FREQS, SHARE, 256), BF16),
            pltpu.VMEM((HALVES, ROW_TILES, 32, RANK, 256), BF16),
            pltpu.VMEM((HALVES, 64, RANK, 256), BF16),
            dma, dma, dma((ZN,)),
            *[dma((HALVES, ROW_TILES))] * 4,
            *[dma((HALVES, ROW_TILES))] * 3, dma((HALVES, ZN)),
        ],
        compiler_params=pltpu.CompilerParams(
            collective_id=0, has_side_effects=True, vmem_limit_bytes=56 << 20
        ),
        cost_estimate=pl.CostEstimate(flops=9_000_000_000, bytes_accessed=11_000_000, transcendentals=0),
    )(wavefield, row_factors, col_factors, window_index.reshape(1, VP), jnp.asarray(mats))


def solution(mesh):
    in_specs = (
        P("freq", None, "tile", None),
        P("freq", None, "tile", None),
        P("freq", None, "tile", None),
        P(),
    )
    return jax.shard_map(
        functools.partial(local, transform_matrices()),
        mesh=mesh,
        in_specs=in_specs,
        out_specs=P("freq", None, "tile", None),
        check_vma=False,
    )
```

```python
import functools
import math

import jax
import jax.numpy as jnp
import numpy as np
from jax import lax
from jax.experimental import pallas as pl
from jax.experimental.pallas import tpu as pltpu
from jax.sharding import PartitionSpec as P

TS = 512
RANK = 32
NT = 16
FREQS = 8
ZN = 8
XN = 4
VP = 256
LANES = 128
HALVES = 2
ROW_TILES = 2
SHARE = TS // FREQS
GROUP = 4 * ROW_TILES
CHUNKS = [(h, i) for h in range(HALVES) for i in range(ROW_TILES)]
MESH = pl.DeviceIdType.MESH
F32 = jnp.float32
BF16 = jnp.bfloat16


def transform_matrices():
    times, freqs = np.meshgrid(np.arange(NT), np.arange(FREQS), indexing="ij")
    angles = math.pi / NT * (2 * freqs + 1) * times
    eye = np.eye(16)
    forward = np.concatenate([np.kron(0.25 * np.cos(angles), eye), np.kron(-0.25 * np.sin(angles), eye)], 1)
    both = np.stack([forward, forward.T])
    high = both.astype(BF16)
    low = (both - high.astype(np.float64)).astype(BF16)
    return np.stack([high, low])


def zdelta(k):
    return jnp.where(k % 2 == 1, (k + 1) // 2, ZN - k // 2)


def dot(left, right):
    return jnp.dot(left, right, preferred_element_type=F32)


def dot_t(left, right):
    return lax.dot_general(left, right, (((0,), (0,)), ((), ())), preferred_element_type=F32)


def turned(pair, sign):
    re, im = pair[:, :LANES], pair[:, LANES:]
    return jnp.concatenate([-im, re] if sign > 0 else [im, -re], 1)


def kernel(
    wave_hbm, row_hbm, col_hbm, index_hbm, mats_hbm, out_ref,
    wave, row, col, index_ref, mats_ref, x_one, x_two,
    c_send, c_recv, y_send, y_recv, f_send, f_recv, r_send, r_recv,
    load_wave, load_row, load_col, load_index, load_mats,
    send_a, send_b, send_c, send_d, recv_a, recv_b, recv_c, recv_d,
):
    me, freq = lax.axis_index("tile"), lax.axis_index("freq")
    my_z, my_y, my_core = me // 4, (me // 2) % 2, me % 2

    def col_load(k):
        z = (my_z + zdelta(k)) % ZN
        columns = pl.ds(pl.multiple_of(z * 256, 256), 256)
        return pltpu.make_async_copy(col_hbm.at[0, :, :, columns], col.at[:, :, columns], load_col.at[k])

    wave_load = pltpu.make_async_copy(wave_hbm.at[0], wave, load_wave)
    row_load = pltpu.make_async_copy(row_hbm.at[0], row, load_row)
    index_load = pltpu.make_async_copy(index_hbm, index_ref, load_index)
    mats_load = pltpu.make_async_copy(mats_hbm, mats_ref, load_mats)
    wave_load.start()
    col_load(1).start()

    def tile_peer(k, q):
        z = (my_z + zdelta(k)) % ZN
        return z * 4 + ((my_y + q // 2) % 2) * 2 + (my_core + q % 2) % 2

    def freq_peer(n):
        return (freq + n) % FREQS

    barrier = pltpu.get_barrier_semaphore()
    def greet(k, carry):
        for q in range(4):
            pl.semaphore_signal(barrier, inc=1, device_id={"tile": tile_peer(ZN - k, q)}, device_id_type=MESH)
        return carry

    lax.fori_loop(1, ZN, greet, 0)
    for q in range(1, 4):
        pl.semaphore_signal(barrier, inc=1, device_id={"tile": tile_peer(0, q)}, device_id_type=MESH)
    for n in range(1, FREQS):
        pl.semaphore_signal(barrier, inc=1, device_id={"freq": freq_peer(n)}, device_id_type=MESH)

    for k in range(2, ZN):
        col_load(k).start()
    col_load(0).start()

    wave_load.wait()
    for h in range(HALVES):
        xr = wave[0, :, h * LANES : (h + 1) * LANES]
        xi = wave[1, :, h * LANES : (h + 1) * LANES]
        x_one[:, 2 * h * LANES : (2 * h + 1) * LANES] = xr
        x_one[:, (2 * h + 1) * LANES : (2 * h + 2) * LANES] = xi
        x_two[:, 2 * h * LANES : (2 * h + 1) * LANES] = xi
        x_two[:, (2 * h + 1) * LANES : (2 * h + 2) * LANES] = -xr

    def copy_a(h, i, peer, k, q):
        return pltpu.make_async_remote_copy(
            src_ref=c_send.at[h, ROW_TILES * peer + i],
            dst_ref=c_recv.at[h, i, me],
            send_sem=send_a.at[h, i],
            recv_sem=recv_a.at[h, i],
            device_id={"tile": peer},
            device_id_type=MESH,
        )

    def copy_d(h, i, peer, k, q):
        return pltpu.make_async_remote_copy(
            src_ref=r_send.at[h, i, peer],
            dst_ref=r_recv.at[h, ROW_TILES * me + i],
            send_sem=send_d.at[h, i],
            recv_sem=recv_d.at[h, my_z],
            device_id={"tile": peer},
            device_id_type=MESH,
        )

    def own_a(h, i):
        return pltpu.make_async_copy(c_send.at[h, ROW_TILES * me + i], c_recv.at[h, i, me], recv_a.at[h, i])

    def own_d(h, i):
        return pltpu.make_async_copy(r_send.at[h, i, me], r_recv.at[h, ROW_TILES * me + i], recv_d.at[h, my_z])

    def copy_b(h, i, n):
        peer = freq_peer(n)
        return pltpu.make_async_remote_copy(
            src_ref=y_send.at[h, i, peer],
            dst_ref=y_recv.at[h, i, freq],
            send_sem=send_b.at[h, i],
            recv_sem=recv_b.at[h, i],
            device_id={"freq": peer},
            device_id_type=MESH,
        )

    def copy_c(h, i, n):
        peer = freq_peer(n)
        return pltpu.make_async_remote_copy(
            src_ref=f_send.at[h, i, peer],
            dst_ref=f_recv.at[h, i, freq],
            send_sem=send_c.at[h, i],
            recv_sem=recv_c.at[h, i],
            device_id={"freq": peer},
            device_id_type=MESH,
        )

    def groups(step):
        for q in range(1, 4):
            step(0, q)

        def body(k, carry):
            for q in range(4):
                step(k, q)
            return carry

        lax.fori_loop(1, ZN, body, 0)

    def project(k):
        z = (my_z + zdelta(k)) % ZN
        columns = pl.ds(pl.multiple_of(z * 256, 256), 256)
        value = dot_t(col[0, :, columns], x_one[...]) + dot_t(col[1, :, columns], x_two[...])
        value = value.astype(BF16)
        for h in range(HALVES):
            c_send[h, pl.ds(GROUP * z, GROUP)] = value[:, 256 * h : 256 * (h + 1)].reshape(GROUP, RANK, 256)

    with jax.named_scope("coeffs_and_send"):

        def send_first(k):
            for q in range(4):
                copy_a(0, 0, tile_peer(k, q), k, q).start()

        col_load(1).wait()
        project(1)
        pl.semaphore_wait(barrier, 31 + 7)
        send_first(1)

        def first(k, carry):
            col_load(k).wait()
            project(k)
            send_first(k)
            return carry

        lax.fori_loop(2, ZN, first, 0)
        col_load(0).wait()
        project(0)
        for q in range(1, 4):
            copy_a(0, 0, tile_peer(0, q), 0, q).start()
        row_load.start()
        index_load.start()
        mats_load.start()

    with jax.named_scope("later_coeffs_send"):
        own_a(0, 0).start()
        for h, i in CHUNKS[1:]:
            groups(lambda k, q: copy_a(h, i, tile_peer(k, q), k, q).start())
            own_a(h, i).start()

    def spectra(h, i):
        if (h, i) == (0, 0):
            row_load.wait()
        pltpu.make_async_copy(c_recv.at[h, i], c_recv.at[h, i], recv_a.at[h, i]).wait()
        c_one = c_recv[h, i].reshape(32 * RANK, 256)
        rows = slice(i * TS, (i + 1) * TS)
        value = dot(row[0, rows], c_one) + dot(row[1, rows], turned(c_one, 1))
        y_send[h, i] = value.astype(BF16).reshape(FREQS, SHARE, 256)
        for n in range(1, FREQS):
            copy_b(h, i, n).start()
        pltpu.make_async_copy(y_send.at[h, i, freq], y_recv.at[h, i, freq], recv_b.at[h, i]).start()

    def window(h, i):
        if (h, i) == (0, 0):
            index_load.wait()
            mats_load.wait()
        pltpu.make_async_copy(y_recv.at[h, i], y_recv.at[h, i], recv_b.at[h, i]).wait()
        times = lax.broadcasted_iota(jnp.int32, (256, LANES), 0) // 16
        kept = times < index_ref[:, h * LANES : (h + 1) * LANES]
        kept = jnp.concatenate([kept.astype(F32)] * 2, 1) > 0.5
        for b in range(2):
            blocks = []
            for u in range(2):
                rows = slice((2 * b + u) * 16, (2 * b + u + 1) * 16)
                block = y_recv[h, i, :, rows].reshape(FREQS * 16, 256)
                blocks.append(jnp.concatenate([block[:, :LANES], block[:, LANES:]], 0))
            block = jnp.concatenate(blocks, 1)
            timed = dot(mats_ref[0, 0], block) + dot(mats_ref[1, 0], block)
            timed = jnp.where(kept, timed, 0.0)
            high = timed.astype(BF16)
            low = (timed - high.astype(F32)).astype(BF16)
            value = dot(mats_ref[0, 1], high) + (dot(mats_ref[1, 1], high) + dot(mats_ref[0, 1], low))
            value = value.astype(BF16)
            for u in range(2):
                rows = slice((2 * b + u) * 16, (2 * b + u + 1) * 16)
                part = value[:, u * LANES : (u + 1) * LANES]
                f_send[h, i, :, rows] = jnp.concatenate([part[:128], part[128:]], 1).reshape(FREQS, 16, 256)
        for n in range(1, FREQS):
            copy_c(h, i, n).start()
        pltpu.make_async_copy(f_send.at[h, i, freq], f_recv.at[h, i, freq], recv_c.at[h, i]).start()

    def returned(h, i):
        pltpu.make_async_copy(f_recv.at[h, i], f_recv.at[h, i], recv_c.at[h, i]).wait()
        f_one = f_recv[h, i].reshape(TS, 256)
        rows = slice(i * TS, (i + 1) * TS)
        value = dot_t(row[0, rows], f_one) + dot_t(row[1, rows], turned(f_one, -1))
        r_send[h, i] = value.astype(BF16).reshape(32, RANK, 256)
        groups(lambda k, q: copy_d(h, i, tile_peer(k, q), k, q).start())
        own_d(h, i).start()

    def adjoint(h):
        def step(z, first):
            held = r_recv.at[h, pl.ds(GROUP * z, GROUP)]
            pltpu.make_async_copy(held, held, recv_d.at[h, z]).wait()
            columns = pl.ds(pl.multiple_of(z * 256, 256), 256)
            r_one = held[...].reshape(256, 256)
            value = dot(col[0, :, columns], r_one) + dot(col[1, :, columns], turned(r_one, 1))
            for c in range(2):
                part = value[:, c * LANES : (c + 1) * LANES]
                old = out_ref[0, c, :, h * LANES : (h + 1) * LANES]
                out_ref[0, c, :, h * LANES : (h + 1) * LANES] = part if first else old + part

        step(my_z, True)

        def body(k, carry):
            step((my_z + zdelta(k)) % ZN, False)
            return carry

        lax.fori_loop(1, ZN, body, 0)

    for step in range(len(CHUNKS) + 2):
        for lag, stage in ((2, returned), (1, window), (0, spectra)):
            if 0 <= step - lag < len(CHUNKS):
                stage(*CHUNKS[step - lag])
    for h in range(HALVES):
        adjoint(h)

    with jax.named_scope("drain"):
        for h, i in CHUNKS:
            sent = r_send.at[h, i, pl.ds(0, 31)]
            pltpu.make_async_copy(sent, sent, send_a.at[h, i]).wait()
            pltpu.make_async_copy(sent, sent, send_d.at[h, i]).wait()
            sent = y_send.at[h, i, pl.ds(0, FREQS - 1)]
            pltpu.make_async_copy(sent, sent, send_b.at[h, i]).wait()
            pltpu.make_async_copy(sent, sent, send_c.at[h, i]).wait()


def local(mats, wavefield, row_factors, col_factors, window_index):
    vmem = pl.BlockSpec(memory_space=pltpu.VMEM)
    hbm = pl.BlockSpec(memory_space=pl.ANY)
    dma = pltpu.SemaphoreType.DMA
    shape = wavefield.shape
    return pl.pallas_call(
        kernel,
        out_shape=pltpu.VMEM(shape, F32),
        in_specs=[hbm] * 5,
        out_specs=vmem,
        scratch_shapes=[
            pltpu.VMEM((2, TS, VP), BF16),
            pltpu.VMEM((2, ROW_TILES * TS, 1024), BF16),
            pltpu.VMEM((2, TS, 2048), BF16),
            pltpu.VMEM((1, VP), jnp.int32),
            pltpu.VMEM((2, 2, 256, 256), BF16),
            pltpu.VMEM((TS, 512), BF16),
            pltpu.VMEM((TS, 512), BF16),
            pltpu.VMEM((HALVES, 64, RANK, 256), BF16),
            pltpu.VMEM((HALVES, ROW_TILES, 32, RANK, 256), BF16),
            pltpu.VMEM((HALVES, ROW_TILES, FREQS, SHARE, 256), BF16),
            pltpu.VMEM((HALVES, ROW_TILES, FREQS, SHARE, 256), BF16),
            pltpu.VMEM((HALVES, ROW_TILES, FREQS, SHARE, 256), BF16),
            pltpu.VMEM((HALVES, ROW_TILES, FREQS, SHARE, 256), BF16),
            pltpu.VMEM((HALVES, ROW_TILES, 32, RANK, 256), BF16),
            pltpu.VMEM((HALVES, 64, RANK, 256), BF16),
            dma, dma, dma((ZN,)), dma, dma,
            *[dma((HALVES, ROW_TILES))] * 4,
            *[dma((HALVES, ROW_TILES))] * 3, dma((HALVES, ZN)),
        ],
        compiler_params=pltpu.CompilerParams(
            collective_id=0, has_side_effects=True, vmem_limit_bytes=56 << 20
        ),
        cost_estimate=pl.CostEstimate(flops=9_000_000_000, bytes_accessed=11_000_000, transcendentals=0),
    )(wavefield, row_factors, col_factors, window_index.reshape(1, VP), jnp.asarray(mats))


def solution(mesh):
    in_specs = (
        P("freq", None, "tile", None),
        P("freq", None, "tile", None),
        P("freq", None, "tile", None),
        P(),
    )
    return jax.shard_map(
        functools.partial(local, transform_matrices()),
        mesh=mesh,
        in_specs=in_specs,
        out_specs=P("freq", None, "tile", None),
        check_vma=False,
    )
```

```python
import functools
import math

import jax
import jax.numpy as jnp
import numpy as np
from jax import lax
from jax.experimental import pallas as pl
from jax.experimental.pallas import tpu as pltpu
from jax.sharding import PartitionSpec as P

TS = 512
RANK = 32
NT = 16
FREQS = 8
ZN = 8
XN = 4
VP = 256
LANES = 128
HALVES = 2
ROW_TILES = 2
SHARE = TS // FREQS
GROUP = 4 * ROW_TILES
CHUNKS = [(h, i) for h in range(HALVES) for i in range(ROW_TILES)]
MESH = pl.DeviceIdType.MESH
F32 = jnp.float32
BF16 = jnp.bfloat16


def transform_matrices():
    times, freqs = np.meshgrid(np.arange(NT), np.arange(FREQS), indexing="ij")
    angles = math.pi / NT * (2 * freqs + 1) * times
    eye = np.eye(16)
    forward = np.concatenate([np.kron(0.25 * np.cos(angles), eye), np.kron(-0.25 * np.sin(angles), eye)], 1)
    both = np.stack([forward, forward.T])
    high = both.astype(BF16)
    low = (both - high.astype(np.float64)).astype(BF16)
    return np.stack([high, low])


def zdelta(k):
    return jnp.where(k % 2 == 1, (k + 1) // 2, ZN - k // 2)


def dot(left, right):
    return jnp.dot(left, right, preferred_element_type=F32)


def dot_t(left, right):
    return lax.dot_general(left, right, (((0,), (0,)), ((), ())), preferred_element_type=F32)


def turned(pair, sign):
    re, im = pair[:, :LANES], pair[:, LANES:]
    return jnp.concatenate([-im, re] if sign > 0 else [im, -re], 1)


def kernel(
    wave_hbm, row_hbm, col_hbm, index_hbm, mats_hbm, out_ref,
    wave, row, col, index_ref, mats_ref, x_one, x_two,
    c_send, c_recv, y_send, y_recv, f_send, f_recv, r_send, r_recv,
    load_wave, load_row, load_col, load_index, load_mats,
    send_a, send_b, send_c, send_d, recv_a, recv_b, recv_c, recv_d,
):
    me, freq = lax.axis_index("tile"), lax.axis_index("freq")
    my_z, my_y, my_core = me // 4, (me // 2) % 2, me % 2

    def col_load(k):
        z = (my_z + zdelta(k)) % ZN
        columns = pl.ds(pl.multiple_of(z * 256, 256), 256)
        return pltpu.make_async_copy(col_hbm.at[0, :, :, columns], col.at[:, :, columns], load_col.at[k])

    wave_load = pltpu.make_async_copy(wave_hbm.at[0], wave, load_wave)
    row_load = pltpu.make_async_copy(row_hbm.at[0], row, load_row)
    index_load = pltpu.make_async_copy(index_hbm, index_ref, load_index)
    mats_load = pltpu.make_async_copy(mats_hbm, mats_ref, load_mats)
    wave_load.start()
    col_load(1).start()

    def tile_peer(k, q):
        z = (my_z + zdelta(k)) % ZN
        return z * 4 + ((my_y + q // 2) % 2) * 2 + (my_core + q % 2) % 2

    def freq_peer(n):
        return (freq + n) % FREQS

    barrier = pltpu.get_barrier_semaphore()
    def greet(k, carry):
        for q in range(4):
            pl.semaphore_signal(barrier, inc=1, device_id={"tile": tile_peer(ZN - k, q)}, device_id_type=MESH)
        return carry

    lax.fori_loop(1, ZN, greet, 0)
    for q in range(1, 4):
        pl.semaphore_signal(barrier, inc=1, device_id={"tile": tile_peer(0, q)}, device_id_type=MESH)
    for n in range(1, FREQS):
        pl.semaphore_signal(barrier, inc=1, device_id={"freq": freq_peer(n)}, device_id_type=MESH)

    for k in range(2, ZN):
        col_load(k).start()
    col_load(0).start()

    wave_load.wait()
    for h in range(HALVES):
        xr = wave[0, :, h * LANES : (h + 1) * LANES]
        xi = wave[1, :, h * LANES : (h + 1) * LANES]
        x_one[:, 2 * h * LANES : (2 * h + 1) * LANES] = xr
        x_one[:, (2 * h + 1) * LANES : (2 * h + 2) * LANES] = xi
        x_two[:, 2 * h * LANES : (2 * h + 1) * LANES] = xi
        x_two[:, (2 * h + 1) * LANES : (2 * h + 2) * LANES] = -xr

    def copy_a(h, i, peer, k, q):
        return pltpu.make_async_remote_copy(
            src_ref=c_send.at[h, ROW_TILES * peer + i],
            dst_ref=c_recv.at[h, i, me],
            send_sem=send_a,
            recv_sem=recv_a.at[h, i],
            device_id={"tile": peer},
            device_id_type=MESH,
        )

    def copy_d(h, i, peer, k, q):
        return pltpu.make_async_remote_copy(
            src_ref=r_send.at[h, i, peer],
            dst_ref=r_recv.at[h, ROW_TILES * me + i],
            send_sem=send_d,
            recv_sem=recv_d.at[my_z if h else ZN],
            device_id={"tile": peer},
            device_id_type=MESH,
        )

    def own_a(h, i):
        return pltpu.make_async_copy(c_send.at[h, ROW_TILES * me + i], c_recv.at[h, i, me], recv_a.at[h, i])

    def own_d(h, i):
        return pltpu.make_async_copy(r_send.at[h, i, me], r_recv.at[h, ROW_TILES * me + i], recv_d.at[my_z if h else ZN])

    def copy_b(h, i, n):
        peer = freq_peer(n)
        return pltpu.make_async_remote_copy(
            src_ref=y_send.at[h, i, peer],
            dst_ref=y_recv.at[h, i, freq],
            send_sem=send_b,
            recv_sem=recv_b.at[h, i],
            device_id={"freq": peer},
            device_id_type=MESH,
        )

    def copy_c(h, i, n):
        peer = freq_peer(n)
        return pltpu.make_async_remote_copy(
            src_ref=f_send.at[h, i, peer],
            dst_ref=f_recv.at[h, i, freq],
            send_sem=send_c,
            recv_sem=recv_c.at[h, i],
            device_id={"freq": peer},
            device_id_type=MESH,
        )

    def groups(step):
        for q in range(1, 4):
            step(0, q)

        def body(k, carry):
            for q in range(4):
                step(k, q)
            return carry

        lax.fori_loop(1, ZN, body, 0)

    def project(k):
        z = (my_z + zdelta(k)) % ZN
        columns = pl.ds(pl.multiple_of(z * 256, 256), 256)
        value = dot_t(col[0, :, columns], x_one[...]) + dot_t(col[1, :, columns], x_two[...])
        value = value.astype(BF16)
        for h in range(HALVES):
            c_send[h, pl.ds(GROUP * z, GROUP)] = value[:, 256 * h : 256 * (h + 1)].reshape(GROUP, RANK, 256)

    with jax.named_scope("coeffs_and_send"):

        def send_first(k):
            for q in range(4):
                copy_a(0, 0, tile_peer(k, q), k, q).start()

        col_load(1).wait()
        project(1)
        pl.semaphore_wait(barrier, 31 + 7)
        send_first(1)

        def first(k, carry):
            col_load(k).wait()
            project(k)
            send_first(k)
            return carry

        lax.fori_loop(2, ZN, first, 0)
        col_load(0).wait()
        project(0)
        for q in range(1, 4):
            copy_a(0, 0, tile_peer(0, q), 0, q).start()
        row_load.start()
        index_load.start()
        mats_load.start()

    with jax.named_scope("later_coeffs_send"):
        own_a(0, 0).start()
        for h, i in CHUNKS[1:]:
            groups(lambda k, q: copy_a(h, i, tile_peer(k, q), k, q).start())
            own_a(h, i).start()

    def spectra(h, i):
        if (h, i) == (0, 0):
            row_load.wait()
        pltpu.make_async_copy(c_recv.at[h, i], c_recv.at[h, i], recv_a.at[h, i]).wait()
        c_one = c_recv[h, i].reshape(32 * RANK, 256)
        rows = slice(i * TS, (i + 1) * TS)
        value = dot(row[0, rows], c_one) + dot(row[1, rows], turned(c_one, 1))
        y_send[h, i] = value.astype(BF16).reshape(FREQS, SHARE, 256)
        for n in range(1, FREQS):
            copy_b(h, i, n).start()
        pltpu.make_async_copy(y_send.at[h, i, freq], y_recv.at[h, i, freq], recv_b.at[h, i]).start()

    def window(h, i):
        if (h, i) == (0, 0):
            index_load.wait()
            mats_load.wait()
        pltpu.make_async_copy(y_recv.at[h, i], y_recv.at[h, i], recv_b.at[h, i]).wait()
        times = lax.broadcasted_iota(jnp.int32, (256, LANES), 0) // 16
        kept = times < index_ref[:, h * LANES : (h + 1) * LANES]
        kept = jnp.concatenate([kept.astype(F32)] * 2, 1) > 0.5
        for b in range(2):
            blocks = []
            for u in range(2):
                rows = slice((2 * b + u) * 16, (2 * b + u + 1) * 16)
                block = y_recv[h, i, :, rows].reshape(FREQS * 16, 256)
                blocks.append(jnp.concatenate([block[:, :LANES], block[:, LANES:]], 0))
            block = jnp.concatenate(blocks, 1)
            timed = dot(mats_ref[0, 0], block) + dot(mats_ref[1, 0], block)
            timed = jnp.where(kept, timed, 0.0)
            high = timed.astype(BF16)
            low = (timed - high.astype(F32)).astype(BF16)
            value = dot(mats_ref[0, 1], high) + (dot(mats_ref[1, 1], high) + dot(mats_ref[0, 1], low))
            value = value.astype(BF16)
            for u in range(2):
                rows = slice((2 * b + u) * 16, (2 * b + u + 1) * 16)
                part = value[:, u * LANES : (u + 1) * LANES]
                f_send[h, i, :, rows] = jnp.concatenate([part[:128], part[128:]], 1).reshape(FREQS, 16, 256)
        for n in range(1, FREQS):
            copy_c(h, i, n).start()
        pltpu.make_async_copy(f_send.at[h, i, freq], f_recv.at[h, i, freq], recv_c.at[h, i]).start()

    def returned(h, i):
        pltpu.make_async_copy(f_recv.at[h, i], f_recv.at[h, i], recv_c.at[h, i]).wait()
        f_one = f_recv[h, i].reshape(TS, 256)
        rows = slice(i * TS, (i + 1) * TS)
        value = dot_t(row[0, rows], f_one) + dot_t(row[1, rows], turned(f_one, -1))
        r_send[h, i] = value.astype(BF16).reshape(32, RANK, 256)
        groups(lambda k, q: copy_d(h, i, tile_peer(k, q), k, q).start())
        own_d(h, i).start()

    def adjoint(h):
        def step(z, first):
            held = r_recv.at[h, pl.ds(GROUP * z, GROUP)]
            if h == 1:
                pltpu.make_async_copy(held, held, recv_d.at[z]).wait()
            columns = pl.ds(pl.multiple_of(z * 256, 256), 256)
            r_one = held[...].reshape(256, 256)
            value = dot(col[0, :, columns], r_one) + dot(col[1, :, columns], turned(r_one, 1))
            for c in range(2):
                part = value[:, c * LANES : (c + 1) * LANES]
                old = out_ref[0, c, :, h * LANES : (h + 1) * LANES]
                out_ref[0, c, :, h * LANES : (h + 1) * LANES] = part if first else old + part

        if h == 0:
            pltpu.make_async_copy(r_recv.at[0], r_recv.at[0], recv_d.at[ZN]).wait()
        step(my_z, True)

        def body(k, carry):
            step((my_z + zdelta(k)) % ZN, False)
            return carry

        lax.fori_loop(1, ZN, body, 0)

    for step in range(len(CHUNKS) + 2):
        for lag, stage in ((2, returned), (1, window), (0, spectra)):
            if 0 <= step - lag < len(CHUNKS):
                stage(*CHUNKS[step - lag])
    adjoint(0)
    sent = c_send.at[:, pl.ds(0, 62)]
    pltpu.make_async_copy(sent, sent, send_a).wait()
    for sem in (send_b, send_c):
        sent = y_send.at[:, :, pl.ds(0, FREQS - 1)]
        pltpu.make_async_copy(sent, sent, sem).wait()
    adjoint(1)
    sent = r_send.at[:, :, pl.ds(0, 31)]
    pltpu.make_async_copy(sent, sent, send_d).wait()


def local(mats, wavefield, row_factors, col_factors, window_index):
    vmem = pl.BlockSpec(memory_space=pltpu.VMEM)
    hbm = pl.BlockSpec(memory_space=pl.ANY)
    dma = pltpu.SemaphoreType.DMA
    shape = wavefield.shape
    return pl.pallas_call(
        kernel,
        out_shape=pltpu.VMEM(shape, F32),
        in_specs=[hbm] * 5,
        out_specs=vmem,
        scratch_shapes=[
            pltpu.VMEM((2, TS, VP), BF16),
            pltpu.VMEM((2, ROW_TILES * TS, 1024), BF16),
            pltpu.VMEM((2, TS, 2048), BF16),
            pltpu.VMEM((1, VP), jnp.int32),
            pltpu.VMEM((2, 2, 256, 256), BF16),
            pltpu.VMEM((TS, 512), BF16),
            pltpu.VMEM((TS, 512), BF16),
            pltpu.VMEM((HALVES, 64, RANK, 256), BF16),
            pltpu.VMEM((HALVES, ROW_TILES, 32, RANK, 256), BF16),
            pltpu.VMEM((HALVES, ROW_TILES, FREQS, SHARE, 256), BF16),
            pltpu.VMEM((HALVES, ROW_TILES, FREQS, SHARE, 256), BF16),
            pltpu.VMEM((HALVES, ROW_TILES, FREQS, SHARE, 256), BF16),
            pltpu.VMEM((HALVES, ROW_TILES, FREQS, SHARE, 256), BF16),
            pltpu.VMEM((HALVES, ROW_TILES, 32, RANK, 256), BF16),
            pltpu.VMEM((HALVES, 64, RANK, 256), BF16),
            dma, dma, dma((ZN,)), dma, dma,
            dma, dma, dma, dma,
            *[dma((HALVES, ROW_TILES))] * 3, dma((ZN + 1,)),
        ],
        compiler_params=pltpu.CompilerParams(
            collective_id=0, has_side_effects=True, vmem_limit_bytes=56 << 20
        ),
        cost_estimate=pl.CostEstimate(flops=9_000_000_000, bytes_accessed=11_000_000, transcendentals=0),
    )(wavefield, row_factors, col_factors, window_index.reshape(1, VP), jnp.asarray(mats))


def solution(mesh):
    in_specs = (
        P("freq", None, "tile", None),
        P("freq", None, "tile", None),
        P("freq", None, "tile", None),
        P(),
    )
    return jax.shard_map(
        functools.partial(local, transform_matrices()),
        mesh=mesh,
        in_specs=in_specs,
        out_specs=P("freq", None, "tile", None),
        check_vma=False,
    )
```

```python
import functools
import math

import jax
import jax.numpy as jnp
import numpy as np
from jax import lax
from jax.experimental import pallas as pl
from jax.experimental.pallas import tpu as pltpu
from jax.sharding import PartitionSpec as P

TS = 512
RANK = 32
NT = 16
FREQS = 8
ZN = 8
XN = 4
VP = 256
LANES = 128
HALVES = 2
ROW_TILES = 2
SHARE = TS // FREQS
GROUP = 4 * ROW_TILES
CHUNKS = [(h, i) for h in range(HALVES) for i in range(ROW_TILES)]
MESH = pl.DeviceIdType.MESH
F32 = jnp.float32
BF16 = jnp.bfloat16


def transform_matrices():
    times, freqs = np.meshgrid(np.arange(NT), np.arange(FREQS), indexing="ij")
    angles = math.pi / NT * (2 * freqs + 1) * times
    eye = np.eye(16)
    forward = np.concatenate([np.kron(0.25 * np.cos(angles), eye), np.kron(-0.25 * np.sin(angles), eye)], 1)
    both = np.stack([forward, forward.T])
    high = both.astype(BF16)
    low = (both - high.astype(np.float64)).astype(BF16)
    return np.stack([high, low])


def zdelta(k):
    return jnp.where(k % 2 == 1, (k + 1) // 2, ZN - k // 2)


def dot(left, right):
    return jnp.dot(left, right, preferred_element_type=F32)


def dot_t(left, right):
    return lax.dot_general(left, right, (((0,), (0,)), ((), ())), preferred_element_type=F32)


def turned(pair, sign):
    re, im = pair[:, :LANES], pair[:, LANES:]
    return jnp.concatenate([-im, re] if sign > 0 else [im, -re], 1)


def kernel(
    wave_hbm, row_hbm, col_hbm, index_hbm, mats_hbm, out_ref,
    wave, row, col, index_ref, mats_ref, x_one, x_two,
    c_send, c_recv, y_send, y_recv, f_send, f_recv, r_send, r_recv,
    load_wave, load_row, load_col, load_index, load_mats,
    send_a, send_b, send_c, send_d, recv_a, recv_b, recv_c, recv_d,
):
    me, freq = lax.axis_index("tile"), lax.axis_index("freq")
    my_z, my_y, my_core = me // 4, (me // 2) % 2, me % 2

    def col_load(k):
        z = (my_z + zdelta(k)) % ZN
        columns = pl.ds(pl.multiple_of(z * 256, 256), 256)
        return pltpu.make_async_copy(col_hbm.at[0, :, :, columns], col.at[:, :, columns], load_col.at[k])

    wave_load = pltpu.make_async_copy(wave_hbm.at[0], wave, load_wave)
    row_load = pltpu.make_async_copy(row_hbm.at[0], row, load_row)
    index_load = pltpu.make_async_copy(index_hbm, index_ref, load_index)
    mats_load = pltpu.make_async_copy(mats_hbm, mats_ref, load_mats)
    wave_load.start()
    col_load(1).start()

    def tile_peer(k, q):
        z = (my_z + zdelta(k)) % ZN
        return z * 4 + ((my_y + q // 2) % 2) * 2 + (my_core + q % 2) % 2

    def freq_peer(n):
        return (freq + n) % FREQS

    barrier = pltpu.get_barrier_semaphore()
    def greet(k, carry):
        for q in range(4):
            pl.semaphore_signal(barrier, inc=1, device_id={"tile": tile_peer(ZN - k, q)}, device_id_type=MESH)
        return carry

    lax.fori_loop(1, ZN, greet, 0)
    for q in range(1, 4):
        pl.semaphore_signal(barrier, inc=1, device_id={"tile": tile_peer(0, q)}, device_id_type=MESH)
    for n in range(1, FREQS):
        pl.semaphore_signal(barrier, inc=1, device_id={"freq": freq_peer(n)}, device_id_type=MESH)

    for k in range(2, ZN):
        col_load(k).start()
    col_load(0).start()

    wave_load.wait()
    for h in range(HALVES):
        xr = wave[0, :, h * LANES : (h + 1) * LANES]
        xi = wave[1, :, h * LANES : (h + 1) * LANES]
        x_one[:, 2 * h * LANES : (2 * h + 1) * LANES] = xr
        x_one[:, (2 * h + 1) * LANES : (2 * h + 2) * LANES] = xi
        x_two[:, 2 * h * LANES : (2 * h + 1) * LANES] = xi
        x_two[:, (2 * h + 1) * LANES : (2 * h + 2) * LANES] = -xr

    def copy_a(h, i, peer, k, q):
        return pltpu.make_async_remote_copy(
            src_ref=c_send.at[h, ROW_TILES * peer + i],
            dst_ref=c_recv.at[h, i, me],
            send_sem=send_a,
            recv_sem=recv_a.at[h, i],
            device_id={"tile": peer},
            device_id_type=MESH,
        )

    def copy_d(h, i, peer, k, q):
        return pltpu.make_async_remote_copy(
            src_ref=r_send.at[h, i, peer],
            dst_ref=r_recv.at[h, ROW_TILES * me + i],
            send_sem=send_d,
            recv_sem=recv_d.at[my_z if h else ZN],
            device_id={"tile": peer},
            device_id_type=MESH,
        )

    def own_a(h, i):
        return pltpu.make_async_copy(c_send.at[h, ROW_TILES * me + i], c_recv.at[h, i, me], recv_a.at[h, i])

    def own_d(h, i):
        return pltpu.make_async_copy(r_send.at[h, i, me], r_recv.at[h, ROW_TILES * me + i], recv_d.at[my_z if h else ZN])

    def copy_b(h, i, n):
        peer = freq_peer(n)
        return pltpu.make_async_remote_copy(
            src_ref=y_send.at[h, i, peer],
            dst_ref=y_recv.at[h, i, freq],
            send_sem=send_b,
            recv_sem=recv_b.at[h, i],
            device_id={"freq": peer},
            device_id_type=MESH,
        )

    def copy_c(h, i, n):
        peer = freq_peer(n)
        return pltpu.make_async_remote_copy(
            src_ref=f_send.at[h, i, peer],
            dst_ref=f_recv.at[h, i, freq],
            send_sem=send_c,
            recv_sem=recv_c.at[h, i],
            device_id={"freq": peer},
            device_id_type=MESH,
        )

    def groups(step):
        def body(k, carry):
            for q in range(4):
                step(k, q)
            return carry

        lax.fori_loop(1, 5, body, 0)
        for q in range(1, 4):
            step(0, q)
        lax.fori_loop(5, ZN, body, 0)

    def project(k):
        z = (my_z + zdelta(k)) % ZN
        columns = pl.ds(pl.multiple_of(z * 256, 256), 256)
        value = dot_t(col[0, :, columns], x_one[...]) + dot_t(col[1, :, columns], x_two[...])
        value = value.astype(BF16)
        for h in range(HALVES):
            c_send[h, pl.ds(GROUP * z, GROUP)] = value[:, 256 * h : 256 * (h + 1)].reshape(GROUP, RANK, 256)

    with jax.named_scope("coeffs_and_send"):

        def send_first(k):
            for q in range(4):
                copy_a(0, 0, tile_peer(k, q), k, q).start()

        col_load(1).wait()
        project(1)
        pl.semaphore_wait(barrier, 31 + 7)
        send_first(1)

        def first(k, carry):
            col_load(k).wait()
            project(k)
            send_first(k)
            return carry

        lax.fori_loop(2, ZN, first, 0)
        col_load(0).wait()
        project(0)
        for q in range(1, 4):
            copy_a(0, 0, tile_peer(0, q), 0, q).start()
        row_load.start()
        index_load.start()
        mats_load.start()

    with jax.named_scope("later_coeffs_send"):
        own_a(0, 0).start()
        for h, i in CHUNKS[1:]:
            groups(lambda k, q: copy_a(h, i, tile_peer(k, q), k, q).start())
            own_a(h, i).start()

    def spectra(h, i):
        if (h, i) == (0, 0):
            row_load.wait()
        pltpu.make_async_copy(c_recv.at[h, i], c_recv.at[h, i], recv_a.at[h, i]).wait()
        c_one = c_recv[h, i].reshape(32 * RANK, 256)
        rows = slice(i * TS, (i + 1) * TS)
        value = dot(row[0, rows], c_one) + dot(row[1, rows], turned(c_one, 1))
        y_send[h, i] = value.astype(BF16).reshape(FREQS, SHARE, 256)
        for n in range(1, FREQS):
            copy_b(h, i, n).start()
        pltpu.make_async_copy(y_send.at[h, i, freq], y_recv.at[h, i, freq], recv_b.at[h, i]).start()

    def window(h, i):
        if (h, i) == (0, 0):
            index_load.wait()
            mats_load.wait()
        pltpu.make_async_copy(y_recv.at[h, i], y_recv.at[h, i], recv_b.at[h, i]).wait()
        times = lax.broadcasted_iota(jnp.int32, (256, LANES), 0) // 16
        kept = times < index_ref[:, h * LANES : (h + 1) * LANES]
        kept = jnp.concatenate([kept.astype(F32)] * 2, 1) > 0.5
        for b in range(2):
            blocks = []
            for u in range(2):
                rows = slice((2 * b + u) * 16, (2 * b + u + 1) * 16)
                block = y_recv[h, i, :, rows].reshape(FREQS * 16, 256)
                blocks.append(jnp.concatenate([block[:, :LANES], block[:, LANES:]], 0))
            block = jnp.concatenate(blocks, 1)
            timed = dot(mats_ref[0, 0], block) + dot(mats_ref[1, 0], block)
            timed = jnp.where(kept, timed, 0.0)
            high = timed.astype(BF16)
            low = (timed - high.astype(F32)).astype(BF16)
            value = dot(mats_ref[0, 1], high) + (dot(mats_ref[1, 1], high) + dot(mats_ref[0, 1], low))
            value = value.astype(BF16)
            for u in range(2):
                rows = slice((2 * b + u) * 16, (2 * b + u + 1) * 16)
                part = value[:, u * LANES : (u + 1) * LANES]
                f_send[h, i, :, rows] = jnp.concatenate([part[:128], part[128:]], 1).reshape(FREQS, 16, 256)
        for n in range(1, FREQS):
            copy_c(h, i, n).start()
        pltpu.make_async_copy(f_send.at[h, i, freq], f_recv.at[h, i, freq], recv_c.at[h, i]).start()

    def returned(h, i):
        pltpu.make_async_copy(f_recv.at[h, i], f_recv.at[h, i], recv_c.at[h, i]).wait()
        f_one = f_recv[h, i].reshape(TS, 256)
        rows = slice(i * TS, (i + 1) * TS)
        value = dot_t(row[0, rows], f_one) + dot_t(row[1, rows], turned(f_one, -1))
        r_send[h, i] = value.astype(BF16).reshape(32, RANK, 256)
        groups(lambda k, q: copy_d(h, i, tile_peer(k, q), k, q).start())
        own_d(h, i).start()

    def adjoint(h):
        def product(z):
            held = r_recv.at[h, pl.ds(GROUP * z, GROUP)]
            columns = pl.ds(pl.multiple_of(z * 256, 256), 256)
            r_one = held[...].reshape(256, 256)
            return dot(col[0, :, columns], r_one) + dot(col[1, :, columns], turned(r_one, 1))

        def arrived(z):
            if h == 1:
                held = r_recv.at[h, pl.ds(GROUP * z, GROUP)]
                pltpu.make_async_copy(held, held, recv_d.at[z]).wait()

        def add(zs, first=False):
            for z in zs:
                arrived(z)
            value = functools.reduce(lambda a, b: a + b, [product(z) for z in zs])
            for c in range(2):
                part = value[:, c * LANES : (c + 1) * LANES]
                old = out_ref[0, c, :, h * LANES : (h + 1) * LANES]
                out_ref[0, c, :, h * LANES : (h + 1) * LANES] = part if first else old + part

        def place(k):
            return (my_z + zdelta(k)) % ZN

        if h == 0:
            pltpu.make_async_copy(r_recv.at[0], r_recv.at[0], recv_d.at[ZN]).wait()
        add([my_z], True)

        def body(k, carry):
            add([place(k)])
            return carry

        lax.fori_loop(1, 6, body, 0)
        add([place(k) for k in range(6, ZN)])

    for step in range(len(CHUNKS) + 2):
        for lag, stage in ((2, returned), (1, window), (0, spectra)):
            if 0 <= step - lag < len(CHUNKS):
                stage(*CHUNKS[step - lag])
    adjoint(0)
    sent = c_send.at[:, pl.ds(0, 62)]
    pltpu.make_async_copy(sent, sent, send_a).wait()
    for sem in (send_b, send_c):
        sent = y_send.at[:, :, pl.ds(0, FREQS - 1)]
        pltpu.make_async_copy(sent, sent, sem).wait()
    adjoint(1)
    sent = r_send.at[:, :, pl.ds(0, 31)]
    pltpu.make_async_copy(sent, sent, send_d).wait()


def local(mats, wavefield, row_factors, col_factors, window_index):
    vmem = pl.BlockSpec(memory_space=pltpu.VMEM)
    hbm = pl.BlockSpec(memory_space=pl.ANY)
    dma = pltpu.SemaphoreType.DMA
    shape = wavefield.shape
    return pl.pallas_call(
        kernel,
        out_shape=pltpu.VMEM(shape, F32),
        in_specs=[hbm] * 5,
        out_specs=vmem,
        scratch_shapes=[
            pltpu.VMEM((2, TS, VP), BF16),
            pltpu.VMEM((2, ROW_TILES * TS, 1024), BF16),
            pltpu.VMEM((2, TS, 2048), BF16),
            pltpu.VMEM((1, VP), jnp.int32),
            pltpu.VMEM((2, 2, 256, 256), BF16),
            pltpu.VMEM((TS, 512), BF16),
            pltpu.VMEM((TS, 512), BF16),
            pltpu.VMEM((HALVES, 64, RANK, 256), BF16),
            pltpu.VMEM((HALVES, ROW_TILES, 32, RANK, 256), BF16),
            pltpu.VMEM((HALVES, ROW_TILES, FREQS, SHARE, 256), BF16),
            pltpu.VMEM((HALVES, ROW_TILES, FREQS, SHARE, 256), BF16),
            pltpu.VMEM((HALVES, ROW_TILES, FREQS, SHARE, 256), BF16),
            pltpu.VMEM((HALVES, ROW_TILES, FREQS, SHARE, 256), BF16),
            pltpu.VMEM((HALVES, ROW_TILES, 32, RANK, 256), BF16),
            pltpu.VMEM((HALVES, 64, RANK, 256), BF16),
            dma, dma, dma((ZN,)), dma, dma,
            dma, dma, dma, dma,
            *[dma((HALVES, ROW_TILES))] * 3, dma((ZN + 1,)),
        ],
        compiler_params=pltpu.CompilerParams(
            collective_id=0, has_side_effects=True, vmem_limit_bytes=56 << 20
        ),
        cost_estimate=pl.CostEstimate(flops=9_000_000_000, bytes_accessed=11_000_000, transcendentals=0),
    )(wavefield, row_factors, col_factors, window_index.reshape(1, VP), jnp.asarray(mats))


def solution(mesh):
    in_specs = (
        P("freq", None, "tile", None),
        P("freq", None, "tile", None),
        P("freq", None, "tile", None),
        P(),
    )
    return jax.shard_map(
        functools.partial(local, transform_matrices()),
        mesh=mesh,
        in_specs=in_specs,
        out_specs=P("freq", None, "tile", None),
        check_vma=False,
    )
```
